32 devices in a mesh: grp: 2 (over x), seq: 16 (over z, y, core).
Axes of the slice: x: 2, y: 2, z: 4, core: 2. Of those that a mesh axis runs over, the one named last changes fastest.
Arguments:
- queries: bfloat16 [4096, 4096], P(('grp', 'seq')), parts along dimension 0, may hold values from -24 to 24
- keys: bfloat16 [4096, 512], P(('grp', 'seq')), parts along dimension 0, may hold values from -9 to 9
- values: bfloat16 [4096, 512], P(('grp', 'seq')), parts along dimension 0, may hold values from -8 to 8
- output_gradient: bfloat16 [4096, 4096], P(('grp', 'seq')), parts along dimension 0, may hold values from -8 to 8
- node_of: int32 [4096], P(('grp', 'seq')), parts along dimension 0, may hold values from 0 to 83, as said below
- parent: int32 [168], P('grp'), parts along dimension 0, may hold values from 0 to 67, as said below
Outputs:
- attended: bfloat16 [4096, 4096], P(('grp', 'seq')), parts along dimension 0
- q_grad: bfloat16 [4096, 4096], P(('grp', 'seq')), parts along dimension 0
- keys_gradient: bfloat16 [4096, 512], P(('grp', 'seq')), parts along dimension 0
- values_gradient: bfloat16 [4096, 512], P(('grp', 'seq')), parts along dimension 0
The draws below stay inside these ranges and needn't reach their ends.
There are 2 independent parts, one for each index of `grp`. The reference program is written for one: setup_inputs(seed, part) draws one part's arguments, and reference() takes and returns one part's arrays. A program takes and returns all parts, laid end to end along the dimension named above; each array names one. Nothing has to cross between parts.
Inputs may be any that keep to these rules, and one draw needn't show every extreme that they name: `node_of`: tokens of one node are consecutive around the cycle; tree t holds the nodes t * 21 to t * 21 + 20, its prompt first, on 512 consecutive positions, and a node's ancestors come before it. All ancestors' tokens of a token lie on its own device or on the 4 devices before it around the cycle, and the last token of every tree has its prompt exactly 4 devices back. A prompt is its own parent; every node is at most two parent steps from its prompt.
All inputs are finite; a program needn't handle non-finite values.
Results may differ from the reference program's by a relative error of at most 0.0083.
Values may be sent and summed in bfloat16 or wider, within the bound.
No kernel may reach another device: no remote copies, remote signals or barrier semaphores. Data moves between devices by JAX's collectives and lax.ppermute only.
A program may use at most 128 MiB of HBM per device.

```python
import jax
import jax.numpy as jnp
from jax import lax

QUERY_HEADS = 32
KEY_VALUE_HEADS = 4
HEAD_WIDTH = 128
DEVICE_TOKENS = 128
REACH = 4
BRANCHES = 4
LEAVES = 16
NODES_TREE = 21
TREES = 4
NODES = 84
TREE_LEN = 512
GROUP_TOKENS = 2048
N_SEQ = 16


def draw_queries(key, part):
    key = jax.random.fold_in(key, 7)
    default_fill = 1.25 * jax.random.truncated_normal(key, -4.0, 4.0, (GROUP_TOKENS, QUERY_HEADS * HEAD_WIDTH), jnp.float32)
    return default_fill.astype(jnp.bfloat16)


def draw_keys(key, part):
    key = jax.random.fold_in(key, 9)
    default_fill = 1.25 * jax.random.truncated_normal(key, -4.0, 4.0, (GROUP_TOKENS, KEY_VALUE_HEADS * HEAD_WIDTH), jnp.float32)
    return default_fill.astype(jnp.bfloat16)


def draw_node_of(key, part):
    key = jax.random.fold_in(key, 3)
    root_key, weight_key, coarse_key, fine_key = jax.random.split(key, 4)
    rest_nodes = NODES_TREE - 1
    root_len = jax.random.randint(root_key, (TREES,), TREE_LEN // 8, TREE_LEN // 2 + 1)
    weights = jax.random.randint(weight_key, (TREES, rest_nodes), 1, 9)
    spare_len = TREE_LEN - root_len - rest_nodes
    shares = 1 + spare_len[:, None] * weights // jnp.sum(weights, axis=1, keepdims=True)
    leftover = TREE_LEN - root_len - jnp.sum(shares, axis=1)
    shares = shares.at[:, rest_nodes - 1].add(leftover)
    lengths = jnp.concatenate([root_len[:, None], shares], axis=1)
    node_ends = jnp.cumsum(lengths, axis=1)
    positions = jnp.arange(TREE_LEN, dtype=jnp.int32)
    local_ids = jnp.sum((positions[None, :, None] >= node_ends[:, None, :rest_nodes]).astype(jnp.int32), axis=2)
    tree_base = jnp.arange(TREES, dtype=jnp.int32)[:, None] * NODES_TREE
    stream = (local_ids + tree_base).reshape(GROUP_TOKENS)
    shift_by = jax.random.randint(coarse_key, (), 0, N_SEQ) * DEVICE_TOKENS + jax.random.randint(fine_key, (), 1, DEVICE_TOKENS)
    source_index = (jnp.arange(GROUP_TOKENS, dtype=jnp.int32) - shift_by) % GROUP_TOKENS
    return stream[source_index].astype(jnp.int32)


def draw_parent(key, part):
    key = jax.random.fold_in(key, 5)
    attached = jax.random.randint(key, (TREES, LEAVES - BRANCHES), 1, BRANCHES + 1)
    first_leaves = jnp.broadcast_to(jnp.arange(1, BRANCHES + 1, dtype=jnp.int32), (TREES, BRANCHES))
    upper = jnp.zeros((TREES, 1 + BRANCHES), jnp.int32)
    local_ids = jnp.concatenate([upper, first_leaves, attached], axis=1)
    tree_base = jnp.arange(TREES, dtype=jnp.int32)[:, None] * NODES_TREE
    return (local_ids + tree_base).reshape(NODES).astype(jnp.int32)


def levels(key, shape, pieces, smallest, largest):
    def one(position, parts):
        heights = jax.random.uniform(jax.random.fold_in(jax.random.fold_in(key, 6), position), (parts,), jnp.float32, smallest / len(pieces), largest / len(pieces))
        return jnp.repeat(jnp.exp(heights), shape[position] // parts).reshape((-1,) + (1,) * (len(shape) - position - 1))

    gain = one(*pieces[0])
    for cut in pieces[1:]:
        gain = gain * one(*cut)
    return gain


def bell_draw(own_key, dims, spread, bound, shards=(), kind=jnp.bfloat16):
    values = jax.random.normal(own_key, dims, jnp.float32) * spread
    if len(shards) > 0:
        values = levels(own_key, dims, shards, -0.22, 0.18) * values
    return jnp.clip(values, min=-bound, max=bound).astype(kind)


def setup_inputs(seed: int = 0, part: int = 0) -> dict:
    seeds = jax.random.split(jax.random.key(seed), 7)
    own_keys = jax.random.split(jax.random.fold_in(seeds[6], part), 7)
    queries = draw_queries(jax.random.fold_in(jax.random.fold_in(seeds[6], part), 71), part)
    keys = draw_keys(jax.random.fold_in(jax.random.fold_in(seeds[6], part), 71), part)
    values = bell_draw(own_keys[2], (GROUP_TOKENS, KEY_VALUE_HEADS * HEAD_WIDTH), 2.0, 8.0, ((0, 16),))
    output_gradient = bell_draw(own_keys[3], (GROUP_TOKENS, QUERY_HEADS * HEAD_WIDTH), 2.0, 8.0, ((0, 16),))
    node_of = draw_node_of(jax.random.fold_in(jax.random.fold_in(seeds[6], part), 71), part)
    parent = draw_parent(jax.random.fold_in(jax.random.fold_in(seeds[6], part), 71), part)
    return dict(queries=queries, keys=keys, values=values, output_gradient=output_gradient, node_of=node_of, parent=parent)


def lineage(nodes, parent):
    parents = parent[nodes]
    return jnp.stack([nodes, parents, parent[parents]], axis=1)


def reference(queries, keys, values, output_gradient, node_of, parent):
    group_share = QUERY_HEADS // KEY_VALUE_HEADS
    inv_root = HEAD_WIDTH ** -0.5
    gathered_queries = queries.reshape(N_SEQ, DEVICE_TOKENS, KEY_VALUE_HEADS, group_share, HEAD_WIDTH)
    gradient_total = output_gradient.reshape(N_SEQ, DEVICE_TOKENS, KEY_VALUE_HEADS, group_share, HEAD_WIDTH)
    gathered_keys = keys.reshape(N_SEQ, DEVICE_TOKENS, KEY_VALUE_HEADS, HEAD_WIDTH)
    gathered_values = values.reshape(N_SEQ, DEVICE_TOKENS, KEY_VALUE_HEADS, HEAD_WIDTH)
    node_all = node_of.reshape(N_SEQ, DEVICE_TOKENS)
    offsets = jnp.arange(REACH + 1, dtype=jnp.int32)
    row_index = jnp.arange(DEVICE_TOKENS, dtype=jnp.int32)
    causal = jnp.logical_or(offsets[None, :, None] > 0, row_index[None, None, :] <= row_index[:, None, None])

    def shard_step(carried, device):
        key_gradient, value_gradient = carried
        window = ((device - offsets) % N_SEQ).astype(jnp.int32)
        query_block_rows = gathered_queries[device].astype(jnp.float32)
        gradient_rows = gradient_total[device].astype(jnp.float32)
        key_block_rows = gathered_keys[window].astype(jnp.float32)
        value_block_rows = gathered_values[window].astype(jnp.float32)
        lineage_rows = lineage(node_all[device], parent)
        key_nodes = node_all[window]
        matched = jnp.any(lineage_rows[:, :, None, None] == key_nodes[None, None, :, :], axis=1)
        visible_pairs = jnp.logical_and(matched, causal)
        raw_scores = jnp.einsum("qhgd,skhd->hgqsk", query_block_rows, key_block_rows) * inv_root
        masked_scores = jnp.where(visible_pairs, raw_scores, -jnp.inf)
        row_max = jnp.max(masked_scores, axis=(3, 4), keepdims=True)
        log_total = row_max + jnp.log(jnp.sum(jnp.exp(masked_scores - row_max), axis=(3, 4), keepdims=True))
        attention = jnp.where(visible_pairs, jnp.exp(masked_scores - log_total), 0.0)
        weights = lax.optimization_barrier(attention.astype(jnp.bfloat16)).astype(jnp.float32)
        context_output = jnp.einsum("hgqsk,skhd->qhgd", weights, value_block_rows)
        prob_grad = jnp.einsum("qhgd,skhd->hgqsk", gradient_rows, value_block_rows)
        row_delta = jnp.sum(gradient_rows * context_output, axis=3).transpose(1, 2, 0)[:, :, :, None, None]
        score_grad = lax.optimization_barrier((attention * (prob_grad - row_delta)).astype(jnp.bfloat16)).astype(jnp.float32)
        query_grad = jnp.einsum("hgqsk,skhd->qhgd", score_grad, key_block_rows) * inv_root
        key_portion = jnp.einsum("hgqsk,qhgd->skhd", score_grad, query_block_rows) * inv_root
        value_portion = jnp.einsum("hgqsk,qhgd->skhd", weights, gradient_rows)
        key_gradient = key_gradient.at[window].add(key_portion)
        value_gradient = value_gradient.at[window].add(value_portion)
        return (key_gradient, value_gradient), (context_output, query_grad)

    zero_gradient = jnp.zeros((N_SEQ, DEVICE_TOKENS, KEY_VALUE_HEADS, HEAD_WIDTH), jnp.float32)
    (key_gradient, value_gradient), (context_output, query_grad) = lax.scan(shard_step, (zero_gradient, zero_gradient), jnp.arange(N_SEQ, dtype=jnp.int32))
    attended = context_output.reshape(GROUP_TOKENS, QUERY_HEADS * HEAD_WIDTH).astype(jnp.bfloat16)
    q_grad = query_grad.reshape(GROUP_TOKENS, QUERY_HEADS * HEAD_WIDTH).astype(jnp.bfloat16)
    keys_gradient = key_gradient.reshape(GROUP_TOKENS, KEY_VALUE_HEADS * HEAD_WIDTH).astype(jnp.bfloat16)
    values_gradient = value_gradient.reshape(GROUP_TOKENS, KEY_VALUE_HEADS * HEAD_WIDTH).astype(jnp.bfloat16)
    return (attended, q_grad, keys_gradient, values_gradient)
```

```python
import functools

import jax
import jax.numpy as jnp
from jax import lax
from jax.experimental import pallas as pl
from jax.experimental.pallas import tpu as pltpu
from jax.sharding import PartitionSpec as P

QUERY_HEADS = 32
KEY_VALUE_HEADS = 4
HEAD_WIDTH = 128
SHARE = QUERY_HEADS // KEY_VALUE_HEADS
SCALE = HEAD_WIDTH**-0.5
LOG2_E = 1.4426950408889634
HIDDEN = -1e30
ID_BASE = 128
ID_ROWS = 16

NT = (((1,), (1,)), ((), ()))
NN = (((1,), (0,)), ((), ()))
TN = (((0,), (0,)), ((), ()))
f32 = jnp.float32
bf16 = jnp.bfloat16
VMEM = pl.BlockSpec(memory_space=pltpu.VMEM)
SMEM = pl.BlockSpec(memory_space=pltpu.SMEM)
PARAMS = pltpu.CompilerParams(vmem_limit_bytes=16 << 20)


def dot(a, b, dims):
    return lax.dot_general(a, b, dims, preferred_element_type=f32)


def heads(ref, first, count):
    w = HEAD_WIDTH
    return jnp.concatenate([ref[:, (first + j) * w : (first + j + 1) * w] for j in range(count)], axis=0)


def blocks(refs, core, group, t):
    c = slice(group * HEAD_WIDTH, (group + 1) * HEAD_WIDTH)
    own, near, near_other, far, sibling, far_other = [r[:t, c] for r in refs]
    last = jnp.where(core == 0, far_other, sibling)
    return jnp.concatenate([own, near, near_other, far, last], axis=0)


def ids_of(ref, t):
    row = ref[t : t + ID_ROWS, :].astype(f32)[:1]
    return row[:, :t] * ID_BASE + row[:, t : 2 * t]


def store_parts(total, group, t, own_ref, near_ref, far_ref, other_ref):
    c = slice(group * HEAD_WIDTH, (group + 1) * HEAD_WIDTH)
    own_ref[:, c] = total[:t]
    near_ref[:, c] = total[t : 2 * t].astype(bf16)
    far_ref[:, c] = total[3 * t : 4 * t].astype(bf16)
    other_ref[:t, c] = total[2 * t : 3 * t].astype(bf16)
    other_ref[t:, c] = total[4 * t :].astype(bf16)


def probs_kernel(core_ref, parent_ref, q_ref, do_ref, k0, k1, k2, k3, k4, k5,
                 p_ref, own_ref, near_ref, far_ref, other_ref, bias_ref):
    t = q_ref.shape[0]
    core = core_ref[0]
    refs = (k0, k1, k2, k3, k4, k5)
    own_ids = ids_of(k0, t)
    node = jnp.broadcast_to(own_ids, (t, t)).T[:, :1]
    parents = parent_ref[...].astype(f32)
    index = lax.broadcasted_iota(jnp.int32, (t, parents.shape[1]), 1).astype(f32)
    up = jnp.sum(jnp.where(index == node, parents, 0.0), axis=1, keepdims=True)
    upper = jnp.sum(jnp.where(index == up, parents, 0.0), axis=1, keepdims=True)
    tok = lax.broadcasted_iota(jnp.int32, (t, t), 0)
    key = lax.broadcasted_iota(jnp.int32, (t, t), 1)
    last_ids = jnp.where(core == 0, ids_of(k5, t), ids_of(k4, t))
    for slot, ids in enumerate((own_ids, ids_of(k1, t), ids_of(k2, t), ids_of(k3, t), last_ids)):
        seen = (ids == node) | (ids == up) | (ids == upper)
        if slot == 0:
            seen = seen & (key <= tok)
        bias_ref[slot * t : (slot + 1) * t, :] = jnp.where(seen, 0.0, HIDDEN).T
    for g in range(KEY_VALUE_HEADS):
        keys = blocks(refs, core, g, t)
        for h in range(g * SHARE, (g + 1) * SHARE, 2):
            bias = bias_ref[...]
            s = dot(keys, heads(q_ref, h, 2), NT) * (SCALE * LOG2_E) + jnp.concatenate([bias, bias], axis=1)
            e = jnp.exp2(s - jnp.max(s, axis=0, keepdims=True))
            inv = 1.0 / jnp.sum(e, axis=0, keepdims=True)
            p_ref[:, h * t : (h + 2) * t] = (e * inv).astype(bf16)
        dv = dot(p_ref[:, g * SHARE * t : (g + 1) * SHARE * t], heads(do_ref, g * SHARE, SHARE), NN)
        store_parts(dv, g, t, own_ref, near_ref, far_ref, other_ref)


def score_grad_kernel(core_ref, p_ref, q_ref, do_ref, v0, v1, v2, v3, v4, v5,
                      ds_ref, own_ref, near_ref, far_ref, other_ref):
    t = q_ref.shape[0]
    core = core_ref[0]
    refs = (v0, v1, v2, v3, v4, v5)
    for g in range(KEY_VALUE_HEADS):
        vals = blocks(refs, core, g, t)
        for h in range(g * SHARE, (g + 1) * SHARE, 2):
            c = slice(h * t, (h + 2) * t)
            dp = dot(vals, heads(do_ref, h, 2), NT)
            p = p_ref[:, c].astype(f32)
            delta = jnp.sum(p * dp, axis=0, keepdims=True)
            ds_ref[:, c] = (p * (dp - delta)).astype(bf16)
        dk = dot(ds_ref[:, g * SHARE * t : (g + 1) * SHARE * t], heads(q_ref, g * SHARE, SHARE), NN) * SCALE
        store_parts(dk, g, t, own_ref, near_ref, far_ref, other_ref)


def rows_kernel(core_ref, p_ref, ds_ref, k0, k1, k2, k3, k4, k5, v0, v1, v2, v3, v4, v5, o_ref, dq_ref):
    t = o_ref.shape[0]
    w = HEAD_WIDTH
    core = core_ref[0]
    for g in range(KEY_VALUE_HEADS):
        keys = blocks((k0, k1, k2, k3, k4, k5), core, g, t)
        vals = blocks((v0, v1, v2, v3, v4, v5), core, g, t)
        for h in range(g * SHARE, (g + 1) * SHARE, 2):
            c = slice(h * t, (h + 2) * t)
            o = dot(vals, p_ref[:, c], TN).astype(bf16)
            dq = (dot(keys, ds_ref[:, c], TN) * SCALE).astype(bf16)
            for j in range(2):
                o_ref[:, (h + j) * w : (h + j + 1) * w] = o[:, j * t : (j + 1) * t].T
                dq_ref[:, (h + j) * w : (h + j + 1) * w] = dq[:, j * t : (j + 1) * t].T


def parts_shapes(t):
    width = KEY_VALUE_HEADS * HEAD_WIDTH
    s = jax.ShapeDtypeStruct
    return [s((t, width), f32), s((t, width), bf16), s((t, width), bf16), s((2 * t, width), bf16)]


def ahead(value, by):
    n = lax.axis_size("seq")
    return lax.ppermute(value, "seq", [(i, (i + by) % n) for i in range(n)])


def swap(value):
    n = lax.axis_size("seq")
    return lax.ppermute(value, "seq", [(i, i ^ 1) for i in range(n)])


def spread(value):
    far = ahead(value, 4)
    near = ahead(value, 2)
    return value, near, swap(near), far, swap(value), swap(far)


def collect(own, near, far, other, first):
    t = own.shape[0]
    got = swap(other).astype(f32)
    near = (near.astype(f32) + got[:t]).astype(bf16)
    far = (far.astype(f32) + jnp.where(first, 0.0, got[t:])).astype(bf16)
    own = own + jnp.where(first, got[t:], 0.0)
    far, near = ahead(far, -4), ahead(near, -2)
    return (own + near.astype(f32) + far.astype(f32)).astype(bf16)


def on_device(queries, keys, values, output_gradient, node_of, parent):
    t = queries.shape[0]
    core = lax.axis_index("seq") % 2
    first = core == 0
    core = core.astype(jnp.int32).reshape(1)
    ids = jnp.concatenate([node_of // ID_BASE, node_of % ID_BASE]).astype(bf16)
    ids = jnp.pad(ids[None], ((0, ID_ROWS - 1), (0, keys.shape[1] - 2 * t)))
    ks = spread(jnp.concatenate([keys, ids], axis=0))
    vs = spread(values)
    s = jax.ShapeDtypeStruct
    grid_shape = s((5 * t, QUERY_HEADS * t), bf16)
    p, *dv = pl.pallas_call(
        probs_kernel,
        name="probs",
        in_specs=[SMEM] + [VMEM] * 9,
        out_specs=[VMEM] * 5,
        out_shape=[grid_shape] + parts_shapes(t),
        scratch_shapes=[pltpu.VMEM((5 * t, t), f32)],
        compiler_params=PARAMS,
    )(core, parent[None], queries, output_gradient, *ks)
    dv = collect(*dv, first)
    ds, *dk = pl.pallas_call(
        score_grad_kernel,
        name="score_grad",
        in_specs=[SMEM] + [VMEM] * 9,
        out_specs=[VMEM] * 5,
        out_shape=[grid_shape] + parts_shapes(t),
        compiler_params=PARAMS,
    )(core, p, queries, output_gradient, *vs)
    dk = collect(*dk, first)
    attended, q_grad = pl.pallas_call(
        rows_kernel,
        name="rows",
        in_specs=[SMEM] + [VMEM] * 14,
        out_specs=[VMEM] * 2,
        out_shape=[s(queries.shape, bf16), s(queries.shape, bf16)],
        compiler_params=PARAMS,
    )(core, p, ds, *ks, *vs)
    return attended, q_grad, dk, dv


def solution(mesh):
    rows = P(("grp", "seq"), None)
    return jax.shard_map(
        on_device,
        mesh=mesh,
        in_specs=(rows, rows, rows, rows, P(("grp", "seq")), P("grp")),
        out_specs=(rows, rows, rows, rows),
        check_vma=False,
    )
```

```python
import functools

import jax
import jax.numpy as jnp
from jax import lax
from jax.experimental import pallas as pl
from jax.experimental.pallas import tpu as pltpu
from jax.sharding import PartitionSpec as P

QUERY_HEADS = 32
KEY_VALUE_HEADS = 4
HEAD_WIDTH = 128
SHARE = QUERY_HEADS // KEY_VALUE_HEADS
SCALE = HEAD_WIDTH**-0.5
LOG2_E = 1.4426950408889634
HIDDEN = -1e30
ID_BASE = 128
ID_ROWS = 16
PAD_ROWS = 32

NT = (((1,), (1,)), ((), ()))
NN = (((1,), (0,)), ((), ()))
TN = (((0,), (0,)), ((), ()))
f32 = jnp.float32
bf16 = jnp.bfloat16
VMEM = pl.BlockSpec(memory_space=pltpu.VMEM)
SMEM = pl.BlockSpec(memory_space=pltpu.SMEM)
HBM = pl.BlockSpec(memory_space=pltpu.HBM)
LIMIT = 8 << 20
SMALL = 2 << 20
S = jax.ShapeDtypeStruct


def call(kernel, name, ins, outs, shapes, scratch=(), cost=None, limit=LIMIT):
    return pl.pallas_call(
        kernel,
        name=name,
        in_specs=ins,
        out_specs=outs,
        out_shape=shapes,
        scratch_shapes=list(scratch),
        compiler_params=pltpu.CompilerParams(vmem_limit_bytes=limit),
        cost_estimate=pl.CostEstimate(flops=cost, bytes_accessed=1, transcendentals=0) if cost else None,
    )


def dot(a, b, dims):
    return lax.dot_general(a, b, dims, preferred_element_type=f32)


def heads(ref, first, count):
    w = HEAD_WIDTH
    return jnp.concatenate([ref[:, (first + j) * w : (first + j + 1) * w] for j in range(count)], axis=0)


def gather_blocks(refs, core, all_ref, t):
    own, near, near_other, far, sibling, far_other = refs
    for slot, ref in enumerate((own, near, near_other, far)):
        all_ref[slot * t : (slot + 1) * t, :] = ref[:t, :]
    all_ref[4 * t :, :] = jnp.where(core == 0, far_other[:t, :], sibling[:t, :])


def ids_of(ref, t):
    row = ref[t : t + ID_ROWS, :].astype(f32)[:1]
    return row[:, :t] * ID_BASE + row[:, t : 2 * t]


def store_parts(total, group, t, own_ref, near_ref, far_ref, other_ref, last_ref):
    c = slice(group * HEAD_WIDTH, (group + 1) * HEAD_WIDTH)
    own_ref[:, c] = total[:t]
    near_ref[:, c] = total[t : 2 * t].astype(bf16)
    far_ref[:, c] = total[3 * t : 4 * t].astype(bf16)
    other_ref[:, c] = total[2 * t : 3 * t].astype(bf16)
    last_ref[:, c] = total[4 * t :].astype(bf16)


def lineage_kernel(own_ref, parent_ref, line_ref):
    t = line_ref.shape[0]
    node = jnp.broadcast_to(ids_of(own_ref, t), (t, t)).T[:, :1]
    parents = parent_ref[...].astype(f32)
    index = lax.broadcasted_iota(jnp.int32, (t, parents.shape[1]), 1).astype(f32)
    up = jnp.sum(jnp.where(index == node, parents, 0.0), axis=1, keepdims=True)
    upper = jnp.sum(jnp.where(index == up, parents, 0.0), axis=1, keepdims=True)
    lane = lax.broadcasted_iota(jnp.int32, line_ref.shape, 1)
    line_ref[...] = jnp.where(lane == 0, node, jnp.where(lane == 1, up, upper))


def probs_kernel(core_ref, line_ref, q_ref, do_ref, k0, k1, k2, k3, k4, k5,
                 p_ref, keys_ref, own_ref, near_ref, far_ref, other_ref, last_ref, bias_ref):
    t = line_ref.shape[0]
    core = core_ref[0]
    gather_blocks((k0, k1, k2, k3, k4, k5), core, keys_ref, t)
    node, up, upper = (line_ref[:, j : j + 1] for j in range(3))
    tok = lax.broadcasted_iota(jnp.int32, (t, t), 0)
    key = lax.broadcasted_iota(jnp.int32, (t, t), 1)
    last_ids = jnp.where(core == 0, ids_of(k5, t), ids_of(k4, t))
    for slot, ids in enumerate((ids_of(k0, t), ids_of(k1, t), ids_of(k2, t), ids_of(k3, t), last_ids)):
        seen = (ids == node) | (ids == up) | (ids == upper)
        if slot == 0:
            seen = seen & (key <= tok)
        bias_ref[slot * t : (slot + 1) * t, :] = jnp.where(seen, 0.0, HIDDEN).T
    for g in range(KEY_VALUE_HEADS):
        keys = keys_ref[:, g * HEAD_WIDTH : (g + 1) * HEAD_WIDTH]
        for h in range(g * SHARE, (g + 1) * SHARE, 2):
            bias = bias_ref[...]
            s = dot(keys, heads(q_ref, h, 2), NT) * (SCALE * LOG2_E) + jnp.concatenate([bias, bias], axis=1)
            e = jnp.exp2(s - jnp.max(s, axis=0, keepdims=True))
            inv = 1.0 / jnp.sum(e, axis=0, keepdims=True)
            p_ref[:, h * t : (h + 2) * t] = (e * inv).astype(bf16)
        dv = dot(p_ref[:, g * SHARE * t : (g + 1) * SHARE * t], heads(do_ref, g * SHARE, SHARE), NN)
        store_parts(dv, g, t, own_ref, near_ref, far_ref, other_ref, last_ref)


def score_grad_kernel(core_ref, p_ref, q_ref, do_ref, v0, v1, v2, v3, v4, v5,
                      ds_ref, vals_ref, own_ref, near_ref, far_ref, other_ref, last_ref):
    t = own_ref.shape[0]
    core = core_ref[0]
    gather_blocks((v0, v1, v2, v3, v4, v5), core, vals_ref, t)
    for g in range(KEY_VALUE_HEADS):
        vals = vals_ref[:, g * HEAD_WIDTH : (g + 1) * HEAD_WIDTH]
        for h in range(g * SHARE, (g + 1) * SHARE, 2):
            c = slice(h * t, (h + 2) * t)
            dp = dot(vals, heads(do_ref, h, 2), NT)
            p = p_ref[:, c].astype(f32)
            delta = jnp.sum(p * dp, axis=0, keepdims=True)
            ds_ref[:, c] = (p * (dp - delta)).astype(bf16)
        dk = dot(ds_ref[:, g * SHARE * t : (g + 1) * SHARE * t], heads(q_ref, g * SHARE, SHARE), NN) * SCALE
        store_parts(dk, g, t, own_ref, near_ref, far_ref, other_ref, last_ref)


def rows_kernel(p_ref, ds_ref, keys_ref, vals_ref, o_ref, dq_ref):
    t = o_ref.shape[0]
    w = HEAD_WIDTH
    for h in range(0, QUERY_HEADS, 2):
        g = slice(h // SHARE * w, (h // SHARE + 1) * w)
        c = slice(h * t, (h + 2) * t)
        o = dot(vals_ref[:, g], p_ref[:, c], TN).astype(bf16)
        dq = (dot(keys_ref[:, g], ds_ref[:, c], TN) * SCALE).astype(bf16)
        for j in range(2):
            o_ref[:, (h + j) * w : (h + j + 1) * w] = o[:, j * t : (j + 1) * t].T
            dq_ref[:, (h + j) * w : (h + j + 1) * w] = dq[:, j * t : (j + 1) * t].T


def merge_kernel(core_ref, own_ref, near_ref, far_ref, got_ref, got_last_ref, own_out, near_out, far_out):
    t = own_ref.shape[0]
    first = core_ref[0] == 0
    last = got_last_ref[...].astype(f32)
    own_out[...] = own_ref[...] + jnp.where(first, last, 0.0)
    near_out[:t, :] = (near_ref[...].astype(f32) + got_ref[...].astype(f32)).astype(bf16)
    far_out[:t, :] = (far_ref[...].astype(f32) + jnp.where(first, 0.0, last)).astype(bf16)
    if near_out.shape[0] > t:
        near_out[t:, :] = jnp.zeros((near_out.shape[0] - t, near_out.shape[1]), bf16)
        far_out[t:, :] = jnp.zeros((near_out.shape[0] - t, near_out.shape[1]), bf16)


def total_kernel(own_ref, near_ref, far_ref, out_ref):
    t = own_ref.shape[0]
    out_ref[...] = (own_ref[...] + near_ref[:t, :].astype(f32) + far_ref[:t, :].astype(f32)).astype(bf16)


def ahead(value, by):
    n = lax.axis_size("seq")
    return lax.ppermute(value, "seq", [(i, (i + by) % n) for i in range(n)])


def swap(value):
    n = lax.axis_size("seq")
    return lax.ppermute(value, "seq", [(i, i ^ 1) for i in range(n)])


def with_ids(keys, node_of):
    t, width = keys.shape
    rows = t + ID_ROWS
    digits = [jnp.broadcast_to(d.astype(bf16), (rows, t)) for d in (node_of >> 7, node_of & (ID_BASE - 1))]
    ids = jnp.pad(digits[0], ((0, 0), (0, width - t))) + jnp.pad(digits[1], ((0, 0), (t, width - 2 * t)))
    row = lax.broadcasted_iota(jnp.int32, (rows, width), 0)
    return jnp.where(row < t, jnp.pad(keys, ((0, ID_ROWS), (0, 0))), ids)


def spread(value):
    far = ahead(value, 4)
    near = ahead(value, 2)
    return value, near, swap(near), far, swap(value), swap(far)


def merge(core, own, near, far, other, last, pad):
    t, width = own.shape
    sent = S((t + pad, width), bf16)
    return call(merge_kernel, "merge", [SMEM] + [VMEM] * 5, [VMEM] * 3, [S((t, width), f32), sent, sent], cost=1, limit=SMALL)(
        core, own, near, far, swap(other), swap(last)
    )


def home(own, near, far):
    near, far = ahead(near, -2), ahead(far, -4)
    return call(total_kernel, "total", [VMEM] * 3, VMEM, S(own.shape, bf16), cost=1, limit=SMALL)(own, near, far)


def on_device(queries, keys, values, output_gradient, node_of, parent):
    t, width = keys.shape
    core = (lax.axis_index("seq") % 2).astype(jnp.int32).reshape(1)
    ks = spread(with_ids(keys, node_of))
    values = jnp.pad(values, ((0, PAD_ROWS), (0, 0)))
    far, near = ahead(values, 4), ahead(values, 2)
    line = call(lineage_kernel, "lineage", [VMEM, VMEM], VMEM, S((t, t), f32), cost=1 << 32, limit=SMALL)(
        ks[0], parent[None]
    )
    parts = [S((t, width), f32)] + [S((t, width), bf16)] * 4
    square = S((5 * t, QUERY_HEADS * t), bf16)
    blocks = S((5 * t, width), bf16)
    p, keys_all, *dv = call(
        probs_kernel,
        "probs",
        [SMEM] + [VMEM] * 9,
        [VMEM] * 7,
        [square, blocks] + parts,
        [pltpu.VMEM((5 * t, t), f32)],
        cost=1,
    )(core, line, queries, output_gradient, *ks)
    dv_own, dv_near, dv_far = merge(core, *dv, PAD_ROWS)
    p, dv_near, dv_far, near, far = lax.optimization_barrier((p, dv_near, dv_far, near, far))
    vs = values, near, swap(near), far, swap(values), swap(far)
    dv = home(dv_own, dv_near, dv_far)
    ds, vals_all, *dk = call(
        score_grad_kernel,
        "score_grad",
        [SMEM] + [VMEM] * 9,
        [VMEM] * 7,
        [square, blocks] + parts,
        cost=1,
    )(core, p, queries, output_gradient, *vs)
    dk_own, dk_near, dk_far = merge(core, *dk, 0)
    ds, dk_near, dk_far, dv = lax.optimization_barrier((ds, dk_near, dk_far, dv))
    dk = home(dk_own, dk_near, dk_far)
    attended, q_grad = call(
        rows_kernel,
        "rows",
        [VMEM] * 4,
        [VMEM] * 2,
        [S(queries.shape, bf16), S(queries.shape, bf16)],
        cost=1 << 32,
    )(p, ds, keys_all, vals_all)
    return attended, q_grad, dk, dv


def solution(mesh):
    rows = P(("grp", "seq"), None)
    return jax.shard_map(
        on_device,
        mesh=mesh,
        in_specs=(rows, rows, rows, rows, P(("grp", "seq")), P("grp")),
        out_specs=(rows, rows, rows, rows),
        check_vma=False,
    )
```

```python
import functools

import jax
import jax.numpy as jnp
from jax import lax
from jax.experimental import pallas as pl
from jax.experimental.pallas import tpu as pltpu
from jax.sharding import PartitionSpec as P

QUERY_HEADS = 32
KEY_VALUE_HEADS = 4
HEAD_WIDTH = 128
SHARE = QUERY_HEADS // KEY_VALUE_HEADS
SCALE = HEAD_WIDTH**-0.5
LOG2_E = 1.4426950408889634
HIDDEN = -1e30
PAD_ROWS = 16
HALF = KEY_VALUE_HEADS // 2

NT = (((1,), (1,)), ((), ()))
NN = (((1,), (0,)), ((), ()))
TN = (((0,), (0,)), ((), ()))
f32 = jnp.float32
bf16 = jnp.bfloat16
VMEM = pl.BlockSpec(memory_space=pltpu.VMEM)
SMEM = pl.BlockSpec(memory_space=pltpu.SMEM)
HBM = pl.BlockSpec(memory_space=pltpu.HBM)
LIMIT = 8 << 20
SMALL = 2 << 20
S = jax.ShapeDtypeStruct


def call(kernel, name, ins, outs, shapes, scratch=(), cost=None, limit=LIMIT):
    return pl.pallas_call(
        kernel,
        name=name,
        in_specs=ins,
        out_specs=outs,
        out_shape=shapes,
        scratch_shapes=list(scratch),
        compiler_params=pltpu.CompilerParams(vmem_limit_bytes=limit),
        cost_estimate=pl.CostEstimate(flops=cost, bytes_accessed=1, transcendentals=0) if cost else None,
    )


def dot(a, b, dims):
    return lax.dot_general(a, b, dims, preferred_element_type=f32)


def heads(ref, first, count):
    w = HEAD_WIDTH
    return jnp.concatenate([ref[:, (first + j) * w : (first + j + 1) * w] for j in range(count)], axis=0)


def gather_blocks(own, near, near_other, far, sibling, far_other, core, all_ref):
    t = all_ref.shape[0] // 5
    for slot, ref in enumerate((own, near, near_other, far)):
        all_ref[slot * t : (slot + 1) * t, :] = ref[:t, :]
    all_ref[4 * t :, :] = jnp.where(core == 0, far_other[:t, :], sibling[:t, :])


def store_parts(total, group, t, refs):
    c = slice(group * HEAD_WIDTH, (group + 1) * HEAD_WIDTH)
    for slot, ref in zip((0, 1, 3, 2, 4), refs):
        ref[:, c] = total[slot * t : (slot + 1) * t].astype(ref.dtype)


def carry_parts(refs, earlier):
    for ref, old in zip(refs, earlier):
        ref[:, : old.shape[1]] = old[...]


def nodes_kernel(node_ref, near_ref, far_ref, out_ref):
    row = lax.broadcasted_iota(jnp.int32, out_ref.shape, 0)
    own, near, far = (jnp.broadcast_to(r[...], out_ref.shape) for r in (node_ref, near_ref, far_ref))
    out_ref[...] = jnp.where(row == 0, own, jnp.where(row == 1, near, far))


def lineage_kernel(node_ref, parent_ref, line_ref):
    t = node_ref.shape[1]
    node = jnp.broadcast_to(node_ref[...].astype(f32), (t, t)).T[:, :1]
    parents = parent_ref[...].astype(f32)
    index = lax.broadcasted_iota(jnp.int32, (t, parents.shape[1]), 1).astype(f32)
    up = jnp.sum(jnp.where(index == node, parents, 0.0), axis=1, keepdims=True)
    upper = jnp.sum(jnp.where(index == up, parents, 0.0), axis=1, keepdims=True)
    lane = lax.broadcasted_iota(jnp.int32, line_ref.shape, 1)
    line_ref[...] = jnp.where(lane == 0, node, jnp.where(lane == 1, up, upper))


def probs_of(groups, keys_ref, bias_ref, q_ref, do_ref, e_ref, scaled_ref, inv_ref, parts):
    t = q_ref.shape[0]
    w = HEAD_WIDTH
    for g in groups:
        keys = keys_ref[:, g * w : (g + 1) * w]
        first = (g - groups[0]) * SHARE
        for h in range(first, first + SHARE, 2):
            bias = bias_ref[...]
            s = dot(keys, heads(q_ref, groups[0] * SHARE + h, 2), NT) * (SCALE * LOG2_E)
            s = s + jnp.concatenate([bias, bias], axis=1)
            e = jnp.exp2(s - jnp.max(s, axis=0, keepdims=True))
            inv = 1.0 / jnp.sum(e, axis=0, keepdims=True)
            e_ref[:, h * t : (h + 2) * t] = e.astype(bf16)
            inv_ref[h : h + 1, :] = inv[:, :t]
            inv_ref[h + 1 : h + 2, :] = inv[:, t:]
        for j in range(first, first + SHARE):
            c = slice((groups[0] * SHARE + j) * w, (groups[0] * SHARE + j + 1) * w)
            column = jnp.broadcast_to(inv_ref[j : j + 1, :], (w, t)).T
            scaled_ref[:, j * w : (j + 1) * w] = (do_ref[:, c].astype(f32) * column).astype(bf16)
        dv = dot(e_ref[:, first * t : (first + SHARE) * t], heads(scaled_ref, first, SHARE), NN)
        store_parts(dv, g, t, parts)


def first_probs_kernel(core_ref, line_ref, q_ref, do_ref, mine_ref, others_ref,
                       k0, k1, k2, k3, k4, k5,
                       e_ref, scaled_ref, inv_ref, keys_ref, bias_ref, *parts):
    t = line_ref.shape[0]
    core = core_ref[0]
    gather_blocks(k0, k1, k2, k3, k4, k5, core, keys_ref)
    mine, others = mine_ref[...].astype(f32), others_ref[...].astype(f32)
    node, up, upper = (line_ref[:, j : j + 1] for j in range(3))
    tok = lax.broadcasted_iota(jnp.int32, (t, t), 0)
    key = lax.broadcasted_iota(jnp.int32, (t, t), 1)
    last_ids = jnp.where(core == 0, others[2:3], others[0:1])
    for slot, ids in enumerate((mine[0:1], mine[1:2], others[1:2], mine[2:3], last_ids)):
        seen = (ids == node) | (ids == up) | (ids == upper)
        if slot == 0:
            seen = seen & (key <= tok)
        bias_ref[slot * t : (slot + 1) * t, :] = jnp.where(seen, 0.0, HIDDEN).T
    probs_of(range(HALF), keys_ref, bias_ref, q_ref, do_ref, e_ref, scaled_ref, inv_ref, parts)


def second_probs_kernel(q_ref, do_ref, keys_ref, bias_ref, *refs):
    earlier, (e_ref, scaled_ref, inv_ref), parts = refs[:5], refs[5:8], refs[8:]
    carry_parts(parts, earlier)
    probs_of(range(HALF, KEY_VALUE_HEADS), keys_ref, bias_ref, q_ref, do_ref, e_ref, scaled_ref, inv_ref, parts)


def score_grads_of(groups, vals_ref, e_ref, scaled_ref, inv_ref, q_ref, ds_ref, context_ref, parts):
    t = q_ref.shape[0]
    w = HEAD_WIDTH
    for g in groups:
        vals = vals_ref[:, g * w : (g + 1) * w]
        first = (g - groups[0]) * SHARE
        for h in range(first, first + SHARE, 2):
            c = slice(h * t, (h + 2) * t)
            e = e_ref[:, c]
            inv = jnp.concatenate([inv_ref[h : h + 1, :], inv_ref[h + 1 : h + 2, :]], axis=1)
            context = dot(vals, e, TN) * inv
            context_ref[:, c] = context.astype(bf16)
            rows = heads(scaled_ref, h, 2)
            delta = jnp.sum(rows.T.astype(f32) * context, axis=0, keepdims=True)
            ds_ref[:, c] = (e.astype(f32) * (dot(vals, rows, NT) - delta)).astype(bf16)
        dk = dot(ds_ref[:, first * t : (first + SHARE) * t], heads(q_ref, g * SHARE, SHARE), NN) * SCALE
        store_parts(dk, g, t, parts)


def first_score_grad_kernel(core_ref, e_ref, scaled_ref, inv_ref, q_ref, v0, v1, v2, v3, v4, v5,
                            ds_ref, context_ref, vals_ref, *parts):
    gather_blocks(v0, v1, v2, v3, v4, v5, core_ref[0], vals_ref)
    score_grads_of(range(HALF), vals_ref, e_ref, scaled_ref, inv_ref, q_ref, ds_ref, context_ref, parts)


def second_score_grad_kernel(e_ref, scaled_ref, inv_ref, q_ref, vals_ref, *refs):
    earlier, (ds_ref, context_ref), parts = refs[:5], refs[5:7], refs[7:]
    carry_parts(parts, earlier)
    groups = range(HALF, KEY_VALUE_HEADS)
    score_grads_of(groups, vals_ref, e_ref, scaled_ref, inv_ref, q_ref, ds_ref, context_ref, parts)


def rows_kernel(c0, c1, ds0, ds1, keys_ref, o_ref, dq_ref):
    t = o_ref.shape[0]
    w = HEAD_WIDTH
    for h in range(0, QUERY_HEADS, 2):
        context_ref, ds_ref = ((c0, ds0), (c1, ds1))[h // (HALF * SHARE)]
        g = slice(h // SHARE * w, (h // SHARE + 1) * w)
        c = slice(h % (HALF * SHARE) * t, (h % (HALF * SHARE) + 2) * t)
        dq = (dot(keys_ref[:, g], ds_ref[:, c], TN) * SCALE).astype(bf16)
        o = context_ref[:, c]
        for j in range(2):
            o_ref[:, (h + j) * w : (h + j + 1) * w] = o[:, j * t : (j + 1) * t].T
            dq_ref[:, (h + j) * w : (h + j + 1) * w] = dq[:, j * t : (j + 1) * t].T


def merge_kernel(core_ref, own_ref, near_ref, far_ref, got_ref, got_last_ref, own_out, near_out, far_out):
    first = core_ref[0] == 0
    last = got_last_ref[...].astype(f32)
    own_out[...] = own_ref[...] + jnp.where(first, last, 0.0)
    t = own_ref.shape[0]
    near_out[:t, :] = (near_ref[...].astype(f32) + got_ref[...].astype(f32)).astype(bf16)
    far_out[:t, :] = (far_ref[...].astype(f32) + jnp.where(first, 0.0, last)).astype(bf16)
    for out in (near_out, far_out):
        if out.shape[0] > t:
            out[t:, :] = jnp.zeros((out.shape[0] - t, out.shape[1]), bf16)


def total_kernel(own_ref, near_ref, far_ref, out_ref):
    t = own_ref.shape[0]
    out_ref[...] = (own_ref[...] + near_ref[:t, :].astype(f32) + far_ref[:t, :].astype(f32)).astype(bf16)


def ahead(value, by):
    n = lax.axis_size("seq")
    return lax.ppermute(value, "seq", [(i, (i + by) % n) for i in range(n)])


def swap(value):
    n = lax.axis_size("seq")
    return lax.ppermute(value, "seq", [(i, i ^ 1) for i in range(n)])


def merge(core, own, near, far, got, got_last, pad=0):
    sent = S((near.shape[0] + pad, near.shape[1]), bf16)
    return call(
        merge_kernel, "merge", [SMEM] + [VMEM] * 5, [VMEM] * 3, [S(own.shape, f32), sent, sent], cost=1, limit=SMALL
    )(core, own, near, far, got, got_last)


def home(own, near, far, cost=1):
    far, near = ahead(far, -4), ahead(near, -2)
    return call(total_kernel, "total", [VMEM] * 3, VMEM, S(own.shape, bf16), cost=cost, limit=SMALL)(own, near, far)


def on_device(queries, keys, values, output_gradient, node_of, parent):
    t, width = keys.shape
    core = (lax.axis_index("seq") % 2).astype(jnp.int32).reshape(1)
    node = node_of[None]
    near, far = ahead(keys, 2), ahead(keys, 4)
    near_node, far_node = ahead(node, 2), ahead(node, 4)
    line = call(lineage_kernel, "lineage", [VMEM, VMEM], VMEM, S((t, t), f32), cost=1 << 32, limit=SMALL)(
        node, parent[None]
    )
    mine = call(nodes_kernel, "nodes", [VMEM] * 3, VMEM, S((8, t), jnp.int32), cost=1, limit=SMALL)(
        node, near_node, far_node
    )
    own, _ = lax.optimization_barrier((keys, line))
    ks = (keys, near, swap(near), far, swap(own), swap(far))
    values = jnp.pad(values, ((0, PAD_ROWS), (0, 0)))
    far, near = ahead(values, 4), ahead(values, 2)
    parts = [S((t, width), f32)] + [S((t, width), bf16)] * 4
    half_parts = [S((t, HALF * HEAD_WIDTH), p.dtype) for p in parts]
    square = S((5 * t, HALF * SHARE * t), bf16)
    blocks = S((5 * t, width), bf16)
    scaled = S((t, HALF * SHARE * HEAD_WIDTH), bf16)
    inv = S((HALF * SHARE, t), f32)
    e0, scaled0, inv0, keys_all, bias, *dv = call(
        first_probs_kernel,
        "first_probs",
        [SMEM] + [VMEM] * 11,
        [VMEM] * 10,
        [square, scaled, inv, blocks, S((5 * t, t), f32)] + half_parts,
        cost=1,
    )(core, line, queries, output_gradient, mine, swap(mine), *ks)
    dv[0], near, far = lax.optimization_barrier((dv[0], near, far))
    near_other, sibling, far_other = swap(near), swap(values), swap(far)
    e1, scaled1, inv1, *dv = call(
        second_probs_kernel, "second_probs", [VMEM] * 9, [VMEM] * 8, [square, scaled, inv] + parts, cost=1
    )(queries, output_gradient, keys_all, bias, *dv)
    near_other, sibling, far_other, e1, e0 = lax.optimization_barrier((near_other, sibling, far_other, e1, e0))
    context = S((HEAD_WIDTH, HALF * SHARE * t), bf16)
    ds0, context0, vals_all, *dk = call(
        first_score_grad_kernel,
        "first_score_grad",
        [SMEM] + [VMEM] * 10,
        [VMEM] * 8,
        [square, context, blocks] + half_parts,
        cost=1,
    )(core, e0, scaled0, inv0, queries, values, near, near_other, far, sibling, far_other)
    got, got_last, ds0 = lax.optimization_barrier((swap(dv[3]), swap(dv[4]), ds0))
    dv_own, dv_near, dv_far = merge(core, *dv[:3], got, got_last, PAD_ROWS)
    dk[0], dv_near, dv_far = lax.optimization_barrier((dk[0], dv_near, dv_far))
    dv = home(dv_own, dv_near, dv_far)
    ds1, context1, *dk = call(
        second_score_grad_kernel, "second_score_grad", [VMEM] * 10, [VMEM] * 7, [square, context] + parts, cost=1
    )(e1, scaled1, inv1, queries, vals_all, *dk)
    dk_own, dk_near, dk_far = merge(core, *dk[:3], swap(dk[3]), swap(dk[4]))
    ds0, ds1, dk_near, dk_far = lax.optimization_barrier((ds0, ds1, dk_near, dk_far))
    dk = home(dk_own, dk_near, dk_far)
    ds0, dv = lax.optimization_barrier((ds0, dv))
    attended, q_grad = call(
        rows_kernel,
        "rows",
        [VMEM] * 5,
        [VMEM] * 2,
        [S(queries.shape, bf16), S(queries.shape, bf16)],
        cost=1 << 32,
    )(context0, context1, ds0, ds1, keys_all)
    return attended, q_grad, dk, dv


def solution(mesh):
    rows = P(("grp", "seq"), None)
    return jax.shard_map(
        on_device,
        mesh=mesh,
        in_specs=(rows, rows, rows, rows, P(("grp", "seq")), P("grp")),
        out_specs=(rows, rows, rows, rows),
        check_vma=False,
    )
```

```python
import functools

import jax
import jax.numpy as jnp
from jax import lax
from jax.experimental import pallas as pl
from jax.experimental.pallas import tpu as pltpu
from jax.sharding import PartitionSpec as P

QUERY_HEADS = 32
KEY_VALUE_HEADS = 4
HEAD_WIDTH = 128
SHARE = QUERY_HEADS // KEY_VALUE_HEADS
SCALE = HEAD_WIDTH**-0.5
LOG2_E = 1.4426950408889634
HIDDEN = -1e30
PAD_ROWS = 16
HALF = KEY_VALUE_HEADS // 2

NT = (((1,), (1,)), ((), ()))
NN = (((1,), (0,)), ((), ()))
TN = (((0,), (0,)), ((), ()))
f32 = jnp.float32
bf16 = jnp.bfloat16
VMEM = pl.BlockSpec(memory_space=pltpu.VMEM)
SMEM = pl.BlockSpec(memory_space=pltpu.SMEM)
HBM = pl.BlockSpec(memory_space=pltpu.HBM)
LIMIT = 8 << 20
SMALL = 2 << 20
S = jax.ShapeDtypeStruct


def call(kernel, name, ins, outs, shapes, scratch=(), cost=None, limit=LIMIT):
    return pl.pallas_call(
        kernel,
        name=name,
        in_specs=ins,
        out_specs=outs,
        out_shape=shapes,
        scratch_shapes=list(scratch),
        compiler_params=pltpu.CompilerParams(vmem_limit_bytes=limit),
        cost_estimate=pl.CostEstimate(flops=cost, bytes_accessed=1, transcendentals=0) if cost else None,
    )


def dot(a, b, dims):
    return lax.dot_general(a, b, dims, preferred_element_type=f32)


def heads(ref, first, count):
    w = HEAD_WIDTH
    return jnp.concatenate([ref[:, (first + j) * w : (first + j + 1) * w] for j in range(count)], axis=0)


def gather_blocks(own, near, near_other, far, sibling, far_other, core, all_ref):
    t = all_ref.shape[0] // 5
    for slot, ref in enumerate((own, near, near_other, far)):
        all_ref[slot * t : (slot + 1) * t, :] = ref[:t, :]
    all_ref[4 * t :, :] = jnp.where(core == 0, far_other[:t, :], sibling[:t, :])


def store_parts(total, group, t, refs):
    c = slice(group * HEAD_WIDTH, (group + 1) * HEAD_WIDTH)
    for slot, ref in zip((0, 1, 3, 2, 4), refs):
        ref[:, c] = total[slot * t : (slot + 1) * t].astype(ref.dtype)


def carry_parts(refs, earlier):
    for ref, old in zip(refs, earlier):
        ref[:, : old.shape[1]] = old[...]


def nodes_kernel(node_ref, near_ref, far_ref, out_ref):
    row = lax.broadcasted_iota(jnp.int32, out_ref.shape, 0)
    own, near, far = (jnp.broadcast_to(r[...], out_ref.shape) for r in (node_ref, near_ref, far_ref))
    out_ref[...] = jnp.where(row == 0, own, jnp.where(row == 1, near, far))


def lineage_kernel(node_ref, parent_ref, line_ref):
    t = node_ref.shape[1]
    node = jnp.broadcast_to(node_ref[...].astype(f32), (t, t)).T[:, :1]
    parents = parent_ref[...].astype(f32)
    index = lax.broadcasted_iota(jnp.int32, (t, parents.shape[1]), 1).astype(f32)
    up = jnp.sum(jnp.where(index == node, parents, 0.0), axis=1, keepdims=True)
    upper = jnp.sum(jnp.where(index == up, parents, 0.0), axis=1, keepdims=True)
    lane = lax.broadcasted_iota(jnp.int32, line_ref.shape, 1)
    line_ref[...] = jnp.where(lane == 0, node, jnp.where(lane == 1, up, upper))


def probs_of(groups, keys_ref, bias_ref, q_ref, do_ref, e_ref, scaled_ref, inv_ref, parts):
    t = q_ref.shape[0]
    w = HEAD_WIDTH
    for g in groups:
        keys = keys_ref[:, g * w : (g + 1) * w]
        first = (g - groups[0]) * SHARE
        for h in range(first, first + SHARE, 2):
            bias = bias_ref[...]
            s = dot(keys, heads(q_ref, groups[0] * SHARE + h, 2), NT) * (SCALE * LOG2_E)
            s = s + jnp.concatenate([bias, bias], axis=1)
            e = jnp.exp2(s - jnp.max(s, axis=0, keepdims=True))
            inv = 1.0 / jnp.sum(e, axis=0, keepdims=True)
            e_ref[:, h * t : (h + 2) * t] = e.astype(bf16)
            inv_ref[h : h + 1, :] = inv[:, :t]
            inv_ref[h + 1 : h + 2, :] = inv[:, t:]
        for j in range(first, first + SHARE):
            c = slice((groups[0] * SHARE + j) * w, (groups[0] * SHARE + j + 1) * w)
            column = jnp.broadcast_to(inv_ref[j : j + 1, :], (w, t)).T
            scaled_ref[:, j * w : (j + 1) * w] = (do_ref[:, c].astype(f32) * column).astype(bf16)
        dv = dot(e_ref[:, first * t : (first + SHARE) * t], heads(scaled_ref, first, SHARE), NN)
        store_parts(dv, g, t, parts)


def first_probs_kernel(core_ref, line_ref, q_ref, do_ref, mine_ref, others_ref,
                       k0, k1, k2, k3, k4, k5,
                       e_ref, scaled_ref, inv_ref, keys_ref, bias_ref, *parts):
    t = line_ref.shape[0]
    core = core_ref[0]
    gather_blocks(k0, k1, k2, k3, k4, k5, core, keys_ref)
    mine, others = mine_ref[...].astype(f32), others_ref[...].astype(f32)
    node, up, upper = (line_ref[:, j : j + 1] for j in range(3))
    tok = lax.broadcasted_iota(jnp.int32, (t, t), 0)
    key = lax.broadcasted_iota(jnp.int32, (t, t), 1)
    last_ids = jnp.where(core == 0, others[2:3], others[0:1])
    for slot, ids in enumerate((mine[0:1], mine[1:2], others[1:2], mine[2:3], last_ids)):
        seen = (ids == node) | (ids == up) | (ids == upper)
        if slot == 0:
            seen = seen & (key <= tok)
        bias_ref[slot * t : (slot + 1) * t, :] = jnp.where(seen, 0.0, HIDDEN).T
    probs_of(range(HALF), keys_ref, bias_ref, q_ref, do_ref, e_ref, scaled_ref, inv_ref, parts)


def second_probs_kernel(q_ref, do_ref, keys_ref, bias_ref, *refs):
    earlier, (e_ref, scaled_ref, inv_ref), parts = refs[:5], refs[5:8], refs[8:]
    carry_parts(parts, earlier)
    probs_of(range(HALF, KEY_VALUE_HEADS), keys_ref, bias_ref, q_ref, do_ref, e_ref, scaled_ref, inv_ref, parts)


def score_grads_of(groups, vals_ref, e_ref, scaled_ref, inv_ref, q_ref, ds_ref, context_ref, parts):
    t = q_ref.shape[0]
    w = HEAD_WIDTH
    for g in groups:
        vals = vals_ref[:, g * w : (g + 1) * w]
        first = (g - groups[0]) * SHARE
        for h in range(first, first + SHARE, 2):
            c = slice(h * t, (h + 2) * t)
            e = e_ref[:, c]
            inv = jnp.concatenate([inv_ref[h : h + 1, :], inv_ref[h + 1 : h + 2, :]], axis=1)
            context = dot(vals, e, TN) * inv
            context_ref[:, c] = context.astype(bf16)
            rows = heads(scaled_ref, h, 2)
            delta = jnp.sum(rows.T.astype(f32) * context, axis=0, keepdims=True)
            ds_ref[:, c] = (e.astype(f32) * (dot(vals, rows, NT) - delta)).astype(bf16)
        dk = dot(ds_ref[:, first * t : (first + SHARE) * t], heads(q_ref, g * SHARE, SHARE), NN) * SCALE
        store_parts(dk, g, t, parts)


def first_score_grad_kernel(core_ref, e_ref, scaled_ref, inv_ref, q_ref, v0, v1, v2, v3, v4, v5,
                            ds_ref, context_ref, vals_ref, *parts):
    gather_blocks(v0, v1, v2, v3, v4, v5, core_ref[0], vals_ref)
    score_grads_of(range(HALF), vals_ref, e_ref, scaled_ref, inv_ref, q_ref, ds_ref, context_ref, parts)


def second_score_grad_kernel(e_ref, scaled_ref, inv_ref, q_ref, vals_ref, *refs):
    earlier, (ds_ref, context_ref), parts = refs[:5], refs[5:7], refs[7:]
    carry_parts(parts, earlier)
    groups = range(HALF, KEY_VALUE_HEADS)
    score_grads_of(groups, vals_ref, e_ref, scaled_ref, inv_ref, q_ref, ds_ref, context_ref, parts)


def rows_kernel(c0, c1, ds0, ds1, keys_ref, o_ref, dq_ref):
    t = o_ref.shape[0]
    w = HEAD_WIDTH
    for h in range(0, QUERY_HEADS, 2):
        context_ref, ds_ref = ((c0, ds0), (c1, ds1))[h // (HALF * SHARE)]
        g = slice(h // SHARE * w, (h // SHARE + 1) * w)
        c = slice(h % (HALF * SHARE) * t, (h % (HALF * SHARE) + 2) * t)
        dq = (dot(keys_ref[:, g], ds_ref[:, c], TN) * SCALE).astype(bf16)
        o = context_ref[:, c]
        for j in range(2):
            o_ref[:, (h + j) * w : (h + j + 1) * w] = o[:, j * t : (j + 1) * t].T
            dq_ref[:, (h + j) * w : (h + j + 1) * w] = dq[:, j * t : (j + 1) * t].T


def merge_kernel(core_ref, own_ref, near_ref, far_ref, got_ref, got_last_ref, own_out, near_out, far_out):
    first = core_ref[0] == 0
    last = got_last_ref[...].astype(f32)
    own_out[...] = own_ref[...] + jnp.where(first, last, 0.0)
    t = own_ref.shape[0]
    near_out[:t, :] = (near_ref[...].astype(f32) + got_ref[...].astype(f32)).astype(bf16)
    far_out[:t, :] = (far_ref[...].astype(f32) + jnp.where(first, 0.0, last)).astype(bf16)
    for out in (near_out, far_out):
        if out.shape[0] > t:
            out[t:, :] = jnp.zeros((out.shape[0] - t, out.shape[1]), bf16)


def add_kernel(own_ref, part_ref, out_ref):
    t = own_ref.shape[0]
    out_ref[...] = (own_ref[...] + part_ref[:t, :].astype(f32)).astype(out_ref.dtype)


def ahead(value, by):
    n = lax.axis_size("seq")
    return lax.ppermute(value, "seq", [(i, (i + by) % n) for i in range(n)])


def swap(value):
    n = lax.axis_size("seq")
    return lax.ppermute(value, "seq", [(i, i ^ 1) for i in range(n)])


def merge(core, own, near, far, got, got_last, pad=0):
    sent = S((near.shape[0] + pad, near.shape[1]), bf16)
    return call(
        merge_kernel, "merge", [SMEM] + [VMEM] * 5, [VMEM] * 3, [S(own.shape, f32), sent, sent], cost=1, limit=SMALL
    )(core, own, near, far, got, got_last)


def add(own, part, dtype, cost):
    return call(add_kernel, "add", [VMEM] * 2, VMEM, S(own.shape, dtype), cost=cost, limit=SMALL)(own, part)


def home(own, near, far):
    far, near = ahead(far, -4), ahead(near, -2)
    return add(add(own, far, f32, 1 << 26), near, bf16, 1)


def on_device(queries, keys, values, output_gradient, node_of, parent):
    t, width = keys.shape
    core = (lax.axis_index("seq") % 2).astype(jnp.int32).reshape(1)
    node = node_of[None]
    near, far = ahead(keys, 2), ahead(keys, 4)
    near_node, far_node = ahead(node, 2), ahead(node, 4)
    line = call(lineage_kernel, "lineage", [VMEM, VMEM], VMEM, S((t, t), f32), cost=1 << 32, limit=SMALL)(
        node, parent[None]
    )
    mine = call(nodes_kernel, "nodes", [VMEM] * 3, VMEM, S((8, t), jnp.int32), cost=1, limit=SMALL)(
        node, near_node, far_node
    )
    own, _ = lax.optimization_barrier((keys, line))
    ks = (keys, near, swap(near), far, swap(own), swap(far))
    values = jnp.pad(values, ((0, PAD_ROWS), (0, 0)))
    far, near = ahead(values, 4), ahead(values, 2)
    parts = [S((t, width), f32)] + [S((t, width), bf16)] * 4
    half_parts = [S((t, HALF * HEAD_WIDTH), p.dtype) for p in parts]
    square = S((5 * t, HALF * SHARE * t), bf16)
    blocks = S((5 * t, width), bf16)
    scaled = S((t, HALF * SHARE * HEAD_WIDTH), bf16)
    inv = S((HALF * SHARE, t), f32)
    e0, scaled0, inv0, keys_all, bias, *dv = call(
        first_probs_kernel,
        "first_probs",
        [SMEM] + [VMEM] * 11,
        [VMEM] * 10,
        [square, scaled, inv, blocks, S((5 * t, t), f32)] + half_parts,
        cost=1,
    )(core, line, queries, output_gradient, mine, swap(mine), *ks)
    dv[0], near, far = lax.optimization_barrier((dv[0], near, far))
    near_other, sibling, far_other = swap(near), swap(values), swap(far)
    e1, scaled1, inv1, *dv = call(
        second_probs_kernel, "second_probs", [VMEM] * 9, [VMEM] * 8, [square, scaled, inv] + parts, cost=1
    )(queries, output_gradient, keys_all, bias, *dv)
    near_other, sibling, far_other, e1, e0 = lax.optimization_barrier((near_other, sibling, far_other, e1, e0))
    context = S((HEAD_WIDTH, HALF * SHARE * t), bf16)
    ds0, context0, vals_all, *dk = call(
        first_score_grad_kernel,
        "first_score_grad",
        [SMEM] + [VMEM] * 10,
        [VMEM] * 8,
        [square, context, blocks] + half_parts,
        cost=1,
    )(core, e0, scaled0, inv0, queries, values, near, near_other, far, sibling, far_other)
    got, got_last, ds0 = lax.optimization_barrier((swap(dv[3]), swap(dv[4]), ds0))
    dv_own, dv_near, dv_far = merge(core, *dv[:3], got, got_last, PAD_ROWS)
    dk[0], dv_near, dv_far = lax.optimization_barrier((dk[0], dv_near, dv_far))
    dv = home(dv_own, dv_near, dv_far)
    ds1, context1, *dk = call(
        second_score_grad_kernel, "second_score_grad", [VMEM] * 10, [VMEM] * 7, [square, context] + parts, cost=1
    )(e1, scaled1, inv1, queries, vals_all, *dk)
    dk_own, dk_near, dk_far = merge(core, *dk[:3], swap(dk[3]), swap(dk[4]))
    ds0, ds1, dk_near, dk_far = lax.optimization_barrier((ds0, ds1, dk_near, dk_far))
    dk = home(dk_own, dk_near, dk_far)
    ds0, dv = lax.optimization_barrier((ds0, dv))
    attended, q_grad = call(
        rows_kernel,
        "rows",
        [VMEM] * 5,
        [VMEM] * 2,
        [S(queries.shape, bf16), S(queries.shape, bf16)],
        cost=1 << 32,
    )(context0, context1, ds0, ds1, keys_all)
    return attended, q_grad, dk, dv


def solution(mesh):
    rows = P(("grp", "seq"), None)
    return jax.shard_map(
        on_device,
        mesh=mesh,
        in_specs=(rows, rows, rows, rows, P(("grp", "seq")), P("grp")),
        out_specs=(rows, rows, rows, rows),
        check_vma=False,
    )
```

```python
import functools

import jax
import jax.numpy as jnp
from jax import lax
from jax.experimental import pallas as pl
from jax.experimental.pallas import tpu as pltpu
from jax.sharding import PartitionSpec as P

QUERY_HEADS = 32
KEY_VALUE_HEADS = 4
HEAD_WIDTH = 128
SHARE = QUERY_HEADS // KEY_VALUE_HEADS
SCALE = HEAD_WIDTH**-0.5
LOG2_E = 1.4426950408889634
HIDDEN = -1e30
PAD_ROWS = 16
HALF = KEY_VALUE_HEADS // 2

NT = (((1,), (1,)), ((), ()))
NN = (((1,), (0,)), ((), ()))
TN = (((0,), (0,)), ((), ()))
f32 = jnp.float32
bf16 = jnp.bfloat16
VMEM = pl.BlockSpec(memory_space=pltpu.VMEM)
SMEM = pl.BlockSpec(memory_space=pltpu.SMEM)
HBM = pl.BlockSpec(memory_space=pltpu.HBM)
LIMIT = 8 << 20
SMALL = 2 << 20
S = jax.ShapeDtypeStruct


def call(kernel, name, ins, outs, shapes, scratch=(), cost=None, limit=LIMIT):
    return pl.pallas_call(
        kernel,
        name=name,
        in_specs=ins,
        out_specs=outs,
        out_shape=shapes,
        scratch_shapes=list(scratch),
        compiler_params=pltpu.CompilerParams(vmem_limit_bytes=limit),
        cost_estimate=pl.CostEstimate(flops=cost, bytes_accessed=1, transcendentals=0) if cost else None,
    )


def dot(a, b, dims):
    return lax.dot_general(a, b, dims, preferred_element_type=f32)


def heads(ref, first, count):
    w = HEAD_WIDTH
    return jnp.concatenate([ref[:, (first + j) * w : (first + j + 1) * w] for j in range(count)], axis=0)


def gather_blocks(own, near, near_other, far, sibling, far_other, core, all_ref):
    t = all_ref.shape[0] // 5
    for slot, ref in enumerate((own, near, near_other, far)):
        all_ref[slot * t : (slot + 1) * t, :] = ref[:t, :]
    all_ref[4 * t :, :] = jnp.where(core == 0, far_other[:t, :], sibling[:t, :])


def store_parts(total, group, t, refs):
    c = slice(group * HEAD_WIDTH, (group + 1) * HEAD_WIDTH)
    for slot, ref in zip((0, 1, 3, 2, 4), refs):
        ref[:, c] = total[slot * t : (slot + 1) * t].astype(ref.dtype)


def carry_parts(refs, earlier):
    for ref, old in zip(refs, earlier):
        ref[:, : old.shape[1]] = old[...]


def nodes_kernel(node_ref, near_ref, far_ref, out_ref):
    row = lax.broadcasted_iota(jnp.int32, out_ref.shape, 0)
    own, near, far = (jnp.broadcast_to(r[...], out_ref.shape) for r in (node_ref, near_ref, far_ref))
    out_ref[...] = jnp.where(row == 0, own, jnp.where(row == 1, near, far))


def lineage_kernel(node_ref, parent_ref, line_ref):
    t = node_ref.shape[1]
    node = jnp.broadcast_to(node_ref[...].astype(f32), (t, t)).T[:, :1]
    parents = parent_ref[...].astype(f32)
    index = lax.broadcasted_iota(jnp.int32, (t, parents.shape[1]), 1).astype(f32)
    up = jnp.sum(jnp.where(index == node, parents, 0.0), axis=1, keepdims=True)
    upper = jnp.sum(jnp.where(index == up, parents, 0.0), axis=1, keepdims=True)
    lane = lax.broadcasted_iota(jnp.int32, line_ref.shape, 1)
    line_ref[...] = jnp.where(lane == 0, node, jnp.where(lane == 1, up, upper))


def probs_of(groups, keys_ref, bias_ref, q_ref, do_ref, e_ref, scaled_ref, inv_ref, parts):
    t = q_ref.shape[0]
    w = HEAD_WIDTH
    for g in groups:
        keys = keys_ref[:, g * w : (g + 1) * w]
        first = (g - groups[0]) * SHARE
        for h in range(first, first + SHARE, 2):
            bias = bias_ref[...]
            s = dot(keys, heads(q_ref, groups[0] * SHARE + h, 2), NT) * (SCALE * LOG2_E)
            s = s + jnp.concatenate([bias, bias], axis=1)
            e = jnp.exp2(s - jnp.max(s, axis=0, keepdims=True))
            inv = 1.0 / jnp.sum(e, axis=0, keepdims=True)
            e_ref[:, h * t : (h + 2) * t] = e.astype(bf16)
            inv_ref[h : h + 1, :] = inv[:, :t]
            inv_ref[h + 1 : h + 2, :] = inv[:, t:]
        for j in range(first, first + SHARE):
            c = slice((groups[0] * SHARE + j) * w, (groups[0] * SHARE + j + 1) * w)
            column = jnp.broadcast_to(inv_ref[j : j + 1, :], (w, t)).T
            scaled_ref[:, j * w : (j + 1) * w] = (do_ref[:, c].astype(f32) * column).astype(bf16)
        dv = dot(e_ref[:, first * t : (first + SHARE) * t], heads(scaled_ref, first, SHARE), NN)
        store_parts(dv, g, t, parts)


def first_probs_kernel(core_ref, line_ref, q_ref, do_ref, mine_ref, others_ref,
                       k0, k1, k2, k3, k4, k5,
                       e_ref, scaled_ref, inv_ref, keys_ref, bias_ref, *parts):
    t = line_ref.shape[0]
    core = core_ref[0]
    gather_blocks(k0, k1, k2, k3, k4, k5, core, keys_ref)
    mine, others = mine_ref[...].astype(f32), others_ref[...].astype(f32)
    node, up, upper = (line_ref[:, j : j + 1] for j in range(3))
    tok = lax.broadcasted_iota(jnp.int32, (t, t), 0)
    key = lax.broadcasted_iota(jnp.int32, (t, t), 1)
    last_ids = jnp.where(core == 0, others[2:3], others[0:1])
    for slot, ids in enumerate((mine[0:1], mine[1:2], others[1:2], mine[2:3], last_ids)):
        seen = (ids == node) | (ids == up) | (ids == upper)
        if slot == 0:
            seen = seen & (key <= tok)
        bias_ref[slot * t : (slot + 1) * t, :] = jnp.where(seen, 0.0, HIDDEN).T
    probs_of(range(HALF), keys_ref, bias_ref, q_ref, do_ref, e_ref, scaled_ref, inv_ref, parts)


def second_probs_kernel(q_ref, do_ref, keys_ref, bias_ref, *refs):
    earlier, (e_ref, scaled_ref, inv_ref), parts = refs[:5], refs[5:8], refs[8:]
    carry_parts(parts, earlier)
    probs_of(range(HALF, KEY_VALUE_HEADS), keys_ref, bias_ref, q_ref, do_ref, e_ref, scaled_ref, inv_ref, parts)


def score_grads_of(groups, vals_ref, e_ref, scaled_ref, inv_ref, q_ref, ds_ref, context_ref, parts):
    t = q_ref.shape[0]
    w = HEAD_WIDTH
    for g in groups:
        vals = vals_ref[:, g * w : (g + 1) * w]
        first = (g - groups[0]) * SHARE
        for h in range(first, first + SHARE, 2):
            c = slice(h * t, (h + 2) * t)
            e = e_ref[:, c]
            inv = jnp.concatenate([inv_ref[h : h + 1, :], inv_ref[h + 1 : h + 2, :]], axis=1)
            context = dot(vals, e, TN) * inv
            context_ref[:, c] = context.astype(bf16)
            rows = heads(scaled_ref, h, 2)
            delta = jnp.sum(rows.T.astype(f32) * context, axis=0, keepdims=True)
            ds_ref[:, c] = (e.astype(f32) * (dot(vals, rows, NT) - delta)).astype(bf16)
        dk = dot(ds_ref[:, first * t : (first + SHARE) * t], heads(q_ref, g * SHARE, SHARE), NN) * SCALE
        store_parts(dk, g, t, parts)


def first_score_grad_kernel(core_ref, e_ref, scaled_ref, inv_ref, q_ref, v0, v1, v2, v3, v4, v5,
                            ds_ref, context_ref, vals_ref, *parts):
    gather_blocks(v0, v1, v2, v3, v4, v5, core_ref[0], vals_ref)
    score_grads_of(range(HALF), vals_ref, e_ref, scaled_ref, inv_ref, q_ref, ds_ref, context_ref, parts)


def second_score_grad_kernel(e_ref, scaled_ref, inv_ref, q_ref, vals_ref, *refs):
    earlier, (ds_ref, context_ref), parts = refs[:5], refs[5:7], refs[7:]
    carry_parts(parts, earlier)
    groups = range(HALF, KEY_VALUE_HEADS)
    score_grads_of(groups, vals_ref, e_ref, scaled_ref, inv_ref, q_ref, ds_ref, context_ref, parts)


def rows_kernel(c0, c1, ds0, ds1, keys_ref, o_ref, dq_ref):
    t = o_ref.shape[0]
    w = HEAD_WIDTH
    for h in range(0, QUERY_HEADS, 2):
        context_ref, ds_ref = ((c0, ds0), (c1, ds1))[h // (HALF * SHARE)]
        g = slice(h // SHARE * w, (h // SHARE + 1) * w)
        c = slice(h % (HALF * SHARE) * t, (h % (HALF * SHARE) + 2) * t)
        dq = (dot(keys_ref[:, g], ds_ref[:, c], TN) * SCALE).astype(bf16)
        o = context_ref[:, c]
        for j in range(2):
            o_ref[:, (h + j) * w : (h + j + 1) * w] = o[:, j * t : (j + 1) * t].T
            dq_ref[:, (h + j) * w : (h + j + 1) * w] = dq[:, j * t : (j + 1) * t].T


def merge_kernel(core_ref, own_ref, near_ref, far_ref, got_ref, got_last_ref, own_out, near_out, far_out):
    first = core_ref[0] == 0
    last = got_last_ref[...].astype(f32)
    own_out[...] = own_ref[...] + jnp.where(first, last, 0.0)
    t = own_ref.shape[0]
    near_out[:t, :] = (near_ref[...].astype(f32) + got_ref[...].astype(f32)).astype(bf16)
    far_out[:t, :] = (far_ref[...].astype(f32) + jnp.where(first, 0.0, last)).astype(bf16)
    for out in (near_out, far_out):
        if out.shape[0] > t:
            out[t:, :] = jnp.zeros((out.shape[0] - t, out.shape[1]), bf16)


def copy_kernel(in_ref, out_ref):
    out_ref[...] = in_ref[...]


def add_kernel(own_ref, part_ref, out_ref):
    t = own_ref.shape[0]
    out_ref[...] = (own_ref[...] + part_ref[:t, :].astype(f32)).astype(out_ref.dtype)


def ahead(value, by):
    n = lax.axis_size("seq")
    return lax.ppermute(value, "seq", [(i, (i + by) % n) for i in range(n)])


def swap(value):
    n = lax.axis_size("seq")
    return lax.ppermute(value, "seq", [(i, i ^ 1) for i in range(n)])


def merge(core, own, near, far, got, got_last, pad=0):
    sent = S((near.shape[0] + pad, near.shape[1]), bf16)
    return call(
        merge_kernel, "merge", [SMEM] + [VMEM] * 5, [VMEM] * 3, [S(own.shape, f32), sent, sent], cost=1, limit=SMALL
    )(core, own, near, far, got, got_last)


def passed(value, cost=1 << 24):
    return call(copy_kernel, "passed", [VMEM], VMEM, S(value.shape, value.dtype), cost=cost, limit=SMALL)(value)


def add(own, part, dtype, cost):
    return call(add_kernel, "add", [VMEM] * 2, VMEM, S(own.shape, dtype), cost=cost, limit=SMALL)(own, part)


def home(own, near, far):
    far, near = ahead(far, -4), ahead(near, -2)
    return add(add(own, far, f32, 1 << 26), near, bf16, 1)


def on_device(queries, keys, values, output_gradient, node_of, parent):
    t, width = keys.shape
    core = (lax.axis_index("seq") % 2).astype(jnp.int32).reshape(1)
    node = node_of[None]
    near, far = ahead(keys, 2), ahead(keys, 4)
    near_node, far_node = ahead(node, 2), ahead(node, 4)
    line = call(lineage_kernel, "lineage", [VMEM, VMEM], VMEM, S((t, t), f32), cost=1 << 32, limit=SMALL)(
        node, parent[None]
    )
    mine = call(nodes_kernel, "nodes", [VMEM] * 3, VMEM, S((8, t), jnp.int32), cost=1, limit=SMALL)(
        node, near_node, far_node
    )
    own, _ = lax.optimization_barrier((keys, line))
    ks = (keys, near, passed(swap(near)), far, swap(own), swap(far))
    values = jnp.pad(values, ((0, PAD_ROWS), (0, 0)))
    far, near = ahead(values, 4), ahead(values, 2)
    parts = [S((t, width), f32)] + [S((t, width), bf16)] * 4
    half_parts = [S((t, HALF * HEAD_WIDTH), p.dtype) for p in parts]
    square = S((5 * t, HALF * SHARE * t), bf16)
    blocks = S((5 * t, width), bf16)
    scaled = S((t, HALF * SHARE * HEAD_WIDTH), bf16)
    inv = S((HALF * SHARE, t), f32)
    e0, scaled0, inv0, keys_all, bias, *dv = call(
        first_probs_kernel,
        "first_probs",
        [SMEM] + [VMEM] * 11,
        [VMEM] * 10,
        [square, scaled, inv, blocks, S((5 * t, t), f32)] + half_parts,
        cost=1,
    )(core, line, queries, output_gradient, mine, passed(swap(mine), 1 << 30), *ks)
    dv[0], near, far = lax.optimization_barrier((dv[0], near, far))
    near_other, sibling, far_other = swap(near), swap(values), swap(far)
    e1, scaled1, inv1, *dv = call(
        second_probs_kernel, "second_probs", [VMEM] * 9, [VMEM] * 8, [square, scaled, inv] + parts, cost=1
    )(queries, output_gradient, keys_all, bias, *dv)
    near_other, sibling, far_other, e1, e0 = lax.optimization_barrier((near_other, sibling, far_other, e1, e0))
    context = S((HEAD_WIDTH, HALF * SHARE * t), bf16)
    ds0, context0, vals_all, *dk = call(
        first_score_grad_kernel,
        "first_score_grad",
        [SMEM] + [VMEM] * 10,
        [VMEM] * 8,
        [square, context, blocks] + half_parts,
        cost=1,
    )(core, e0, scaled0, inv0, queries, values, near, near_other, far, sibling, far_other)
    got, got_last, ds0 = lax.optimization_barrier((swap(dv[3]), swap(dv[4]), ds0))
    dv_own, dv_near, dv_far = merge(core, *dv[:3], got, got_last, PAD_ROWS)
    dk[0], dv_near, dv_far = lax.optimization_barrier((dk[0], dv_near, dv_far))
    dv = home(dv_own, dv_near, dv_far)
    ds1, context1, *dk = call(
        second_score_grad_kernel, "second_score_grad", [VMEM] * 10, [VMEM] * 7, [square, context] + parts, cost=1
    )(e1, scaled1, inv1, queries, vals_all, *dk)
    dk_own, dk_near, dk_far = merge(core, *dk[:3], swap(dk[3]), swap(dk[4]))
    ds0, ds1, dk_near, dk_far = lax.optimization_barrier((ds0, ds1, dk_near, dk_far))
    dk = home(dk_own, dk_near, dk_far)
    ds0, dv = lax.optimization_barrier((ds0, dv))
    attended, q_grad = call(
        rows_kernel,
        "rows",
        [VMEM] * 5,
        [VMEM] * 2,
        [S(queries.shape, bf16), S(queries.shape, bf16)],
        cost=1 << 32,
    )(context0, context1, ds0, ds1, keys_all)
    return attended, q_grad, dk, dv


def solution(mesh):
    rows = P(("grp", "seq"), None)
    return jax.shard_map(
        on_device,
        mesh=mesh,
        in_specs=(rows, rows, rows, rows, P(("grp", "seq")), P("grp")),
        out_specs=(rows, rows, rows, rows),
        check_vma=False,
    )
```
